32 devices in a mesh: dp: 4 (over y, x), mp: 4 (over z), outer: 2 (over core).
Axes of the slice: x: 2, y: 2, z: 4, core: 2. Of those that a mesh axis runs over, the one named last changes fastest.
Arguments:
- activations: bfloat16 [16384, 8192], P(('dp', 'outer'), 'mp'), may hold values from -6 to 6
- act_scale: float32 [128, 64], P(('dp', 'outer'), 'mp'), may hold values from 0.25 to 4
- out_grads: bfloat16 [16384, 16384], P(('dp', 'outer'), 'mp'), may hold values from -6 to 6
- gradient_tile_scale: float32 [128, 128], P(('dp', 'outer'), 'mp'), may hold values from 0.25 to 4
- prior_input_factor: float32 [8, 1024, 1024], P('mp', ('dp', 'outer')), may hold values from -0.3 to 6, as said below
- g_factor: float32 [16, 1024, 1024], P('mp', ('dp', 'outer')), may hold values from -0.3 to 6, as said below
- weight_grad: bfloat16 [8192, 16384], P('mp', ('dp', 'outer')), may hold values from -6 to 6
- a_inverse: bfloat16 [8, 1024, 1024], P('mp', ('dp', 'outer')), as said below
- g_inverse: bfloat16 [16, 1024, 1024], P(('dp', 'outer'), 'mp'), as said below
Outputs:
- a_stat: float32 [8, 1024, 1024], P('mp', ('dp', 'outer'))
- g_stat: float32 [16, 1024, 1024], P('mp', ('dp', 'outer'))
- new_a_factor: float32 [8, 1024, 1024], P('mp', ('dp', 'outer'))
- new_g_factor: float32 [16, 1024, 1024], P('mp', ('dp', 'outer'))
- preconditioned: bfloat16 [8192, 16384], P('mp', ('dp', 'outer'))
The draws below stay inside these ranges and needn't reach their ends.
Inputs may be any that keep to these rules, and one draw needn't show every extreme that they name: `a_inverse`: each block is the identity plus dense off-diagonal and diagonal entries of magnitude at most 1.5 / sqrt(1024). `g_inverse`: each block is the identity plus dense off-diagonal and diagonal entries of magnitude at most 1.5 / sqrt(1024). `prior_input_factor`: each block is symmetric with a positive diagonal. `g_factor`: each block is symmetric with a positive diagonal.
All inputs are finite; a program needn't handle non-finite values.
Results may differ from the reference program's by a relative error of at most 0.014.
Values may be sent and summed in bfloat16 or wider, within the bound.
No kernel may reach another device: no remote copies, remote signals or barrier semaphores. Data moves between devices by JAX's collectives and lax.ppermute only.
A program may use at most 128 MiB of HBM per device.

```python
import math
import jax
import jax.numpy as jnp
from jax import lax

D = 8192
HID = 16384
BLK = 1024
QT = 128
TOKENS = 16384


def inverse_blocks(key, block_count):
    limit = 1.5 / math.sqrt(BLK)
    spread_part = jnp.clip(jax.random.normal(key, (block_count, BLK, BLK), jnp.float32) * (0.5 / math.sqrt(BLK)), -limit, limit)
    identity = jnp.eye(BLK, dtype=jnp.float32)
    return (identity[None, :, :] + spread_part).astype(jnp.bfloat16)


def factor_blocks(key, block_count):
    level = (16.0 - 1.0 / 16.0) / (4.0 * math.log(4.0))
    diag_key, off_key = jax.random.split(key)
    diag_part = level * jax.random.uniform(diag_key, (block_count, BLK), jnp.float32, 0.6, 1.6)
    raw = jnp.clip(jax.random.normal(off_key, (block_count, BLK, BLK), jnp.float32) * 0.05, -0.2, 0.2)
    symmetric = (raw + jnp.transpose(raw, (0, 2, 1))) * 0.7
    identity = jnp.eye(BLK, dtype=jnp.float32)
    off_part = symmetric * (1.0 - identity)[None, :, :]
    return off_part + identity[None, :, :] * diag_part[:, :, None]


def draw_a_inverse(key, part):
    return inverse_blocks(jax.random.fold_in(key, 11), D // BLK)


def draw_g_inverse(key, part):
    return inverse_blocks(jax.random.fold_in(key, 23), HID // BLK)


def draw_prior_input_factor(key, part):
    return factor_blocks(jax.random.fold_in(key, 37), D // BLK)


def draw_g_factor(key, part):
    return factor_blocks(jax.random.fold_in(key, 41), HID // BLK)


def levels(own_key, extent, pieces, least, top_value):
    level, own = 1.0, jax.random.fold_in(own_key, 6)
    for axis_at, shards_of in pieces:
        heights = jnp.exp(jax.random.uniform(jax.random.fold_in(own, axis_at), (shards_of,), jnp.float32, least / len(pieces), top_value / len(pieces)))
        level = level * jnp.repeat(heights, extent[axis_at] // shards_of).reshape([-1 if axis == axis_at else 1 for axis in range(len(extent))])
    return level


def scatter_about(own_key, dims, scale, most, cuts=(), kind=jnp.bfloat16):
    level = levels(own_key, dims, cuts, -0.22, 0.18) if cuts else 1.0
    entries = jax.random.normal(own_key, dims, jnp.float32) * scale * level
    return jnp.minimum(jnp.maximum(entries, -most), most).astype(kind)


def setup_inputs(seed: int = 0) -> dict:
    splits = jax.random.split(jax.random.key(seed), 10)
    activations = scatter_about(splits[0], (TOKENS, D), 1.0, 6.0, ((0, 8), (1, 4)))
    act_scale = jnp.clip(jnp.exp(math.log(4.0) - 2.7725887 * jax.random.uniform(splits[1], (TOKENS // QT, D // QT), jnp.float32) ** levels(splits[1], (TOKENS // QT, D // QT), ((0, 8), (1, 4)), -0.2, 0.2)), 0.25, 4.0)
    out_grads = scatter_about(splits[2], (TOKENS, HID), 1.0, 6.0, ((0, 8), (1, 4)))
    gradient_tile_scale = jnp.clip(jnp.exp(math.log(4.0) - 2.7725887 * jax.random.uniform(splits[3], (TOKENS // QT, HID // QT), jnp.float32) ** levels(splits[3], (TOKENS // QT, HID // QT), ((0, 8), (1, 4)), -0.2, 0.2)), 0.25, 4.0)
    prior_input_factor = draw_prior_input_factor(jax.random.fold_in(splits[9], 71), 0)
    g_factor = draw_g_factor(jax.random.fold_in(splits[9], 71), 0)
    weight_grad = scatter_about(splits[6], (D, HID), 1.0, 6.0, ((0, 4), (1, 8)))
    a_inverse = draw_a_inverse(jax.random.fold_in(splits[9], 71), 0)
    g_inverse = draw_g_inverse(jax.random.fold_in(splits[9], 71), 0)
    return {"activations": activations, "act_scale": act_scale, "out_grads": out_grads, "gradient_tile_scale": gradient_tile_scale, "prior_input_factor": prior_input_factor, "g_factor": g_factor, "weight_grad": weight_grad, "a_inverse": a_inverse, "g_inverse": g_inverse}


EMA_DECAY = 0.95


def dequantize(quantized, tile_scale):
    row_total, column_total = quantized.shape
    tiles_with_scale = quantized.astype(jnp.float32).reshape(row_total // QT, QT, column_total // QT, QT) * tile_scale[:, None, :, None]
    return tiles_with_scale.reshape(row_total, column_total).astype(jnp.bfloat16)


def block_grams(unscaled_values):
    blocks = unscaled_values.reshape(unscaled_values.shape[0], -1, BLK).transpose(1, 0, 2)

    def one_gram(block):
        wide = block.astype(jnp.float32)
        return jnp.dot(wide.T, wide, precision=lax.Precision.HIGHEST, preferred_element_type=jnp.float32)

    return lax.map(one_gram, blocks)


def reference(activations, act_scale, out_grads, gradient_tile_scale, prior_input_factor, g_factor, weight_grad, a_inverse, g_inverse):
    a_deq = dequantize(activations, act_scale)
    g_deq = dequantize(out_grads, gradient_tile_scale)
    a_stat = block_grams(a_deq) / TOKENS
    g_stat = block_grams(g_deq) / TOKENS
    new_a_factor = EMA_DECAY * prior_input_factor + (1.0 - EMA_DECAY) * a_stat
    new_g_factor = EMA_DECAY * g_factor + (1.0 - EMA_DECAY) * g_stat
    grad_blocks = weight_grad.reshape(D // BLK, BLK, HID // BLK, BLK).astype(jnp.float32)
    right = jnp.einsum("aigk,gkl->aigl", grad_blocks, g_inverse.astype(jnp.float32), precision=lax.Precision.HIGHEST).astype(jnp.bfloat16)
    result = jnp.einsum("aij,ajgl->aigl", a_inverse.astype(jnp.float32), right.astype(jnp.float32), precision=lax.Precision.HIGHEST).astype(jnp.bfloat16)
    return a_stat, g_stat, new_a_factor, new_g_factor, result.reshape(D, HID)
```

```python
import jax
import jax.numpy as jnp
from jax import lax
from jax.experimental import pallas as pl
from jax.experimental.pallas import tpu as pltpu
from jax.sharding import PartitionSpec as P

BLK = 1024
QT = 128
EMA_DECAY = 0.95
BF = jnp.bfloat16
F32 = jnp.float32
VMEM_LIMIT = 48 * 1024 * 1024


def dequantize(quantized, tile_scale):
    rows, columns = quantized.shape
    tiles = (
        quantized.reshape(rows // QT, QT, columns // QT, QT).astype(F32)
        * tile_scale[:, None, :, None]
    )
    return tiles.reshape(rows, columns).astype(BF)


def position(chip, my_chip, bits, order):
    relative = jnp.bitwise_xor(chip, my_chip)
    place = 0
    for bit in order:
        place = place * 2 + jnp.bitwise_and(jnp.right_shift(relative, bit), 1)
    return place


def bit_order(block, bits):
    return [(block + k) % bits for k in range(bits)]


def gram_blocks(where, panel, scale, first, count, chips):
    tokens = panel.shape[0]
    bits = chips.bit_length() - 1
    pair = BLK // chips
    tile = pair // 2
    half = chips // 2
    width = tile * (chips + 1)
    tiles = BLK // QT

    def body(where_ref, scale_ref, x_ref, keep_ref, send_ref, deq):
        step = pl.program_id(0)

        def convert(t, carry):
            rows = pl.ds(pl.multiple_of(t * QT, QT), QT)
            for u in range(tiles):
                value = x_ref[rows, u * QT : (u + 1) * QT].astype(F32)
                value = (value * scale_ref[t, (first + step) * tiles + u]).astype(BF)
                deq[rows, u * QT : (u + 1) * QT] = value
                if u * QT < half * pair:
                    deq[rows, BLK + u * QT : BLK + (u + 1) * QT] = value
            return carry

        lax.fori_loop(0, tokens // QT, convert, 0, unroll=2)
        order_even = bit_order(0, bits)
        order_odd = bit_order(1, bits)
        far = []
        for chip in range(chips):
            span = half * pair + (pair if chip < half else 0)
            start = chip * pair
            sums = lax.dot_general(
                deq[:, start : start + pair],
                deq[:, start : start + span],
                (((0,), (0,)), ((), ())),
                preferred_element_type=F32,
            )
            near = sums[:, : half * pair].astype(BF)
            if chip < half:
                last = sums[:, half * pair :]
                far.append(last)
            else:
                last = jnp.transpose(far[chip - half])
            last = last.astype(BF)
            place = jnp.where(
                (first + step) % 2 == 0,
                position(chip, where_ref[0], bits, order_even),
                position(chip, where_ref[0], bits, order_odd),
            )

            def store(ref, core, near=near, last=last, place=place):
                cut = near.shape[1] - core * tile
                ref[0, place, :, :cut] = near[core * tile : (core + 1) * tile, core * tile :]
                ref[0, place, :, cut:] = last[core * tile : (core + 1) * tile, : (core + 1) * tile]

            @pl.when(where_ref[1] == 0)
            def _():
                store(keep_ref, 0)
                store(send_ref, 1)

            @pl.when(where_ref[1] == 1)
            def _():
                store(keep_ref, 1)
                store(send_ref, 0)

    shape = jax.ShapeDtypeStruct((count, chips, tile, width), BF)
    spec = pl.BlockSpec((1, chips, tile, width), lambda b: (b, 0, 0, 0))
    return pl.pallas_call(
        body,
        grid=(count,),
        out_shape=(shape, shape),
        in_specs=[
            pl.BlockSpec(memory_space=pltpu.SMEM),
            pl.BlockSpec(memory_space=pltpu.SMEM),
            pl.BlockSpec((tokens, BLK), lambda b: (0, first + b)),
        ],
        out_specs=(spec, spec),
        scratch_shapes=[pltpu.VMEM((tokens, BLK + half * pair), BF)],
        compiler_params=pltpu.CompilerParams(vmem_limit_bytes=VMEM_LIMIT),
        cost_estimate=pl.CostEstimate(
            flops=2 * count * tokens * BLK * width,
            bytes_accessed=2 * count * (tokens * BLK + 2 * chips * tile * width),
            transcendentals=0,
        ),
    )(where, scale, panel)


def swap(value, axis, size, bit):
    return lax.ppermute(value, axis, [(i, i ^ (1 << bit)) for i in range(size)])


def scatter_sums(keep, send, first, chips):
    bits = chips.bit_length() - 1
    got = lax.ppermute(send, "outer", [(0, 1), (1, 0)])
    left, right = [], []
    for b in range(keep.shape[0]):
        held, came = keep[b], got[b]
        for bit in bit_order(first + b, bits):
            size = held.shape[0] // 2
            away = (held[size:].astype(F32) + came[size:].astype(F32)).astype(BF)
            came_next = swap(away, "dp", chips, bit)
            held = (held[:size].astype(F32) + came[:size].astype(F32)).astype(BF)
            came = came_next
        left.append(held[0])
        right.append(came[0])
    return left, right


def symmetric_statistics(activations, act_scale, out_grads, gradient_tile_scale, prior_input_factor, g_factor):
    chips = lax.axis_size("dp")
    devices = 2 * chips
    tile = BLK // devices
    token_total = activations.shape[0] * devices
    where = jnp.stack([lax.axis_index("dp"), lax.axis_index("outer")]).astype(jnp.int32)
    inputs = activations.shape[1] // BLK
    hidden = out_grads.shape[1] // BLK
    left, right = [], []
    for panel, scale, total in ((out_grads, gradient_tile_scale, hidden), (activations, act_scale, inputs)):
        for first in range(0, total, 2):
            keep, send = gram_blocks(where, panel, scale, first, min(2, total - first), chips)
            some_left, some_right = scatter_sums(keep, send, first, chips)
            left += some_left
            right += some_right
    left, right = jnp.stack(left), jnp.stack(right)
    mirrored = []
    for k in range(1, chips):
        columns = slice(k * tile, (k + 1) * tile)
        sent = (left[:, :, columns].astype(F32) + right[:, :, columns].astype(F32)).astype(BF)
        mirrored.append(
            lax.ppermute(sent, ("dp", "outer"), [(i, (i + k) % devices) for i in range(devices)])
        )

    def finish(prior, low):
        count = prior.shape[0]

        def body(where_ref, prior_ref, left_ref, right_ref, *rest):
            mirror_refs, stat_ref, new_ref = rest[: chips - 1], rest[-2], rest[-1]
            me = where_ref[0] * 2 + where_ref[1]

            def put(at, sums):
                columns = pl.ds(pl.multiple_of(lax.rem(me + at, devices) * tile, tile), tile)
                stat = sums * (1.0 / token_total)
                stat_ref[0, :, columns] = stat
                new_ref[0, :, columns] = EMA_DECAY * prior_ref[0, :, columns] + (1.0 - EMA_DECAY) * stat

            for k in range(chips + 1):
                columns = slice(k * tile, (k + 1) * tile)
                put(k, left_ref[0, :, columns].astype(F32) + right_ref[0, :, columns].astype(F32))
            for k in range(1, chips):
                put(devices - k, jnp.transpose(mirror_refs[k - 1][0].astype(F32)))

        rows = pl.BlockSpec((1, tile, BLK), lambda b: (b, 0, 0))
        part = pl.BlockSpec((1, tile, tile * (chips + 1)), lambda b: (low + b, 0, 0))
        square = pl.BlockSpec((1, tile, tile), lambda b: (low + b, 0, 0))
        shape = jax.ShapeDtypeStruct((count, tile, BLK), F32)
        return pl.pallas_call(
            body,
            grid=(count,),
            out_shape=(shape, shape),
            in_specs=[pl.BlockSpec(memory_space=pltpu.SMEM), rows, part, part] + [square] * (chips - 1),
            out_specs=(rows, rows),
            compiler_params=pltpu.CompilerParams(vmem_limit_bytes=VMEM_LIMIT),
        )(where, prior, left, right, *mirrored)

    g_stat, new_g_factor = finish(g_factor, 0)
    a_stat, new_a_factor = finish(prior_input_factor, hidden)
    return a_stat, g_stat, new_a_factor, new_g_factor


def plain_statistics(activations, act_scale, out_grads, gradient_tile_scale, prior_input_factor, g_factor):
    a_tiles = dequantize(activations, act_scale).reshape(activations.shape[0], -1, BLK)
    g_tiles = dequantize(out_grads, gradient_tile_scale).reshape(out_grads.shape[0], -1, BLK)
    inputs = a_tiles.shape[1]
    tiles = jnp.concatenate([a_tiles, g_tiles], axis=1)
    rows = jnp.einsum("qym,qyx->myx", tiles, tiles, preferred_element_type=F32)
    summed = lax.psum_scatter(
        rows.astype(BF), ("dp", "outer"), scatter_dimension=0, tiled=True
    ).astype(F32)
    token_total = activations.shape[0] * lax.axis_size("dp") * lax.axis_size("outer")
    statistics = jnp.transpose(summed, (1, 0, 2)) / token_total
    a_stat, g_stat = statistics[:inputs], statistics[inputs:]
    new_a_factor = EMA_DECAY * prior_input_factor + (1.0 - EMA_DECAY) * a_stat
    new_g_factor = EMA_DECAY * g_factor + (1.0 - EMA_DECAY) * g_stat
    return a_stat, g_stat, new_a_factor, new_g_factor


def left_product(a_blocks, weight_grad):
    rows, columns = weight_grad.shape

    def body(a_ref, w_ref, o_ref):
        o_ref[...] = jnp.dot(a_ref[0], w_ref[...], preferred_element_type=F32).astype(BF)

    return pl.pallas_call(
        body,
        grid=(rows // BLK, columns // BLK),
        out_shape=jax.ShapeDtypeStruct((rows, columns), BF),
        in_specs=[
            pl.BlockSpec((1, BLK, BLK), lambda i, j: (i, 0, 0)),
            pl.BlockSpec((BLK, BLK), lambda i, j: (i, j)),
        ],
        out_specs=pl.BlockSpec((BLK, BLK), lambda i, j: (i, j)),
        compiler_params=pltpu.CompilerParams(vmem_limit_bytes=VMEM_LIMIT),
        cost_estimate=pl.CostEstimate(
            flops=2 * rows * columns * BLK,
            bytes_accessed=4 * rows * columns + 2 * rows * BLK,
            transcendentals=0,
        ),
    )(a_blocks, weight_grad)


def chain_slices(own, size):
    before, after = [own], [own]
    for hop in range(1, size):
        before.append(lax.ppermute(before[-1], "mp", [(i, i + 1) for i in range(hop - 1, size - 1)]))
        after.append(lax.ppermute(after[-1], "mp", [(i, i - 1) for i in range(1, size - hop + 1)]))
    return before, after[1:]


def right_product(me, left, before, after, block, target):
    rows, columns = left.shape
    size = len(before)
    depth = before[0].shape[0]
    height = min(512, rows)

    def body(me_ref, left_ref, *rest):
        before_refs, after_refs = rest[:size], rest[size : 2 * size - 1]
        o_ref, whole, sem = rest[-3:]

        @pl.when(pl.program_id(0) == 0)
        def _():
            mine = me_ref[0]

            def fetch(ref, owner):
                rows_of = pl.ds(pl.multiple_of(owner * depth, depth), depth)
                pltpu.make_async_copy(ref, whole.at[rows_of], sem).start()

            fetch(before_refs[0], mine)
            for hop in range(1, size):
                pl.when(mine >= hop)(lambda hop=hop: fetch(before_refs[hop], mine - hop))
                pl.when(mine + hop < size)(lambda hop=hop: fetch(after_refs[hop - 1], mine + hop))
            pltpu.make_async_copy(whole, whole, sem).wait()

        o_ref[...] = jnp.dot(left_ref[...], whole[...], preferred_element_type=F32).astype(BF)

    operands = [me, left, *before, *after]
    specs = [
        pl.BlockSpec(memory_space=pltpu.SMEM),
        pl.BlockSpec((height, BLK), lambda r: (r, block)),
    ] + [pl.BlockSpec(memory_space=pl.ANY)] * (2 * size - 1)
    aliases = {}
    if target is not None:
        aliases = {len(operands): 0}
        operands.append(target)
        specs.append(pl.BlockSpec(memory_space=pl.ANY))
    return pl.pallas_call(
        body,
        grid=(rows // height,),
        out_shape=jax.ShapeDtypeStruct((rows, columns), BF),
        in_specs=specs,
        out_specs=pl.BlockSpec((height, BLK), lambda r: (r, block)),
        scratch_shapes=[pltpu.VMEM((BLK, BLK), BF), pltpu.SemaphoreType.DMA],
        input_output_aliases=aliases,
        compiler_params=pltpu.CompilerParams(vmem_limit_bytes=VMEM_LIMIT),
        cost_estimate=pl.CostEstimate(
            flops=2 * rows * BLK * BLK,
            bytes_accessed=4 * rows * BLK + 2 * BLK * BLK,
            transcendentals=0,
        ),
    )(*operands)


def body(
    activations,
    act_scale,
    out_grads,
    gradient_tile_scale,
    prior_input_factor,
    g_factor,
    weight_grad,
    a_inverse,
    g_inverse,
):
    slices = lax.axis_size("mp")
    chains = [chain_slices(g_inverse[b], slices) for b in range(g_inverse.shape[0])]
    a_blocks = lax.all_gather(a_inverse, ("dp", "outer"), axis=1, tiled=True)
    left = left_product(a_blocks, weight_grad)

    chips = lax.axis_size("dp")
    symmetric = (
        lax.axis_size("outer") == 2
        and chips >= 2
        and chips & (chips - 1) == 0
        and BLK // (2 * chips) % QT == 0
    )
    statistics = symmetric_statistics if symmetric else plain_statistics
    stats = statistics(
        activations, act_scale, out_grads, gradient_tile_scale, prior_input_factor, g_factor
    )

    me = lax.axis_index("mp").astype(jnp.int32).reshape(1)
    result = None
    for block, (before, after) in enumerate(chains):
        result = right_product(me, left, before, after, block, result)
    return (*stats, result)


def solution(mesh):
    return jax.shard_map(
        body,
        mesh=mesh,
        in_specs=(
            P(("dp", "outer"), "mp"),
            P(("dp", "outer"), "mp"),
            P(("dp", "outer"), "mp"),
            P(("dp", "outer"), "mp"),
            P("mp", ("dp", "outer"), None),
            P("mp", ("dp", "outer"), None),
            P("mp", ("dp", "outer")),
            P("mp", ("dp", "outer"), None),
            P(("dp", "outer"), "mp", None),
        ),
        out_specs=(
            P("mp", ("dp", "outer"), None),
            P("mp", ("dp", "outer"), None),
            P("mp", ("dp", "outer"), None),
            P("mp", ("dp", "outer"), None),
            P("mp", ("dp", "outer")),
        ),
        check_vma=False,
    )
```

```python
import jax
import jax.numpy as jnp
from jax import lax
from jax.experimental import pallas as pl
from jax.experimental.pallas import tpu as pltpu
from jax.sharding import PartitionSpec as P

BLK = 1024
QT = 128
EMA_DECAY = 0.95
BF = jnp.bfloat16
F32 = jnp.float32
VMEM_LIMIT = 60 * 1024 * 1024


def dequantize(quantized, tile_scale):
    rows, columns = quantized.shape
    tiles = (
        quantized.reshape(rows // QT, QT, columns // QT, QT).astype(F32)
        * tile_scale[:, None, :, None]
    )
    return tiles.reshape(rows, columns).astype(BF)


def order_after(operands, specs, after):
    for value in after:
        operands.append(value)
        specs.append(pl.BlockSpec(memory_space=pl.ANY))
    return operands, specs


def gram_blocks(where, panels, scales, blocks, chips, after):
    tokens = panels[0].shape[0]
    pair = BLK // chips
    tile = pair // 2
    half = chips // 2
    width = tile * (chips + 1)
    count = len(blocks)
    parts = chips if tokens % (chips * QT) == 0 else 1
    depth = tokens // parts
    wide = BLK + half * pair

    def body(where_ref, *rest):
        scale_refs, panel_refs = rest[:2], rest[2:4]
        keep_hbm, send_hbm, raw, rows_out, in_sems, out_sems = rest[4 + len(after) : -2]
        deq = rest[-2:]

        def incoming(n, part):
            panel, block = blocks[n]
            return pltpu.make_async_copy(
                panel_refs[panel].at[pl.ds(part * depth, depth), pl.ds(block * BLK, BLK)],
                raw.at[n, pl.ds(part * depth, depth)],
                in_sems.at[n, part],
            )

        def outgoing(n):
            return (
                pltpu.make_async_copy(rows_out.at[0, n], keep_hbm.at[:, n], out_sems.at[n, 0]),
                pltpu.make_async_copy(rows_out.at[1, n], send_hbm.at[:, n], out_sems.at[n, 1]),
            )

        def convert(n, part):
            panel, block = blocks[n]
            into = deq[n % 2]
            for t in range(part * depth // QT, (part + 1) * depth // QT):
                rows = slice(t * QT, (t + 1) * QT)
                for u in range(BLK // QT):
                    factor = scale_refs[panel][t, block * (BLK // QT) + u]
                    value = (raw[n, rows, u * QT : (u + 1) * QT].astype(F32) * factor).astype(BF)
                    into[rows, u * QT : (u + 1) * QT] = value
                    if u * QT < wide - BLK:
                        into[rows, BLK + u * QT : BLK + (u + 1) * QT] = value

        for part in range(parts):
            incoming(0, part).start()
        for part in range(parts):
            incoming(0, part).wait()
            convert(0, part)
            if count > 1:
                incoming(1, part).start()
        for n in range(count):
            if 0 < n < count - 1:
                for part in range(parts):
                    incoming(n + 1, part).start()
            source = deq[n % 2]
            far = []
            for chip in range(chips):
                span = half * pair + (pair if chip < half else 0)
                start = chip * pair
                if n + 1 < count and chip < parts:
                    incoming(n + 1, chip).wait()
                sums = lax.dot_general(
                    source[:, start : start + pair],
                    source[:, start : start + span],
                    (((0,), (0,)), ((), ())),
                    preferred_element_type=F32,
                )
                if n + 1 < count and chip < parts:
                    convert(n + 1, chip)
                near = sums[:, : half * pair].astype(BF)
                if chip < half:
                    last = sums[:, half * pair :].astype(BF)
                    far.append(last)
                else:
                    last = jnp.transpose(far[chip - half])
                place = jnp.bitwise_xor(where_ref[0], chip)

                for core in range(2):
                    side = jnp.bitwise_xor(where_ref[1], core)
                    rows = slice(core * tile, (core + 1) * tile)
                    cut = half * pair - core * tile
                    rows_out[side, n, place, :, :cut] = near[rows, core * tile :]
                    rows_out[side, n, place, :, cut:] = last[rows, : (core + 1) * tile]

            for copy in outgoing(n):
                copy.start()
        for n in range(count):
            for copy in outgoing(n):
                copy.wait()

    shape = jax.ShapeDtypeStruct((chips, count, tile, width), BF)
    anywhere = pl.BlockSpec(memory_space=pl.ANY)
    operands, specs = order_after(
        [where, *scales, *panels],
        [pl.BlockSpec(memory_space=pltpu.SMEM)] * 3 + [anywhere] * 2,
        after,
    )
    return pl.pallas_call(
        body,
        out_shape=(shape, shape),
        in_specs=specs,
        out_specs=(anywhere, anywhere),
        scratch_shapes=[
            pltpu.VMEM((count, tokens, BLK), BF),
            pltpu.VMEM((2, count, chips, tile, width), BF),
            pltpu.SemaphoreType.DMA((count, parts)),
            pltpu.SemaphoreType.DMA((count, 2)),
            pltpu.VMEM((tokens, wide), BF),
            pltpu.VMEM((tokens, wide), BF),
        ],
        compiler_params=pltpu.CompilerParams(vmem_limit_bytes=VMEM_LIMIT),
        cost_estimate=pl.CostEstimate(
            flops=int(6.0 * count * tokens * BLK * width),
            bytes_accessed=2 * count * (tokens * BLK + 2 * chips * tile * width),
            transcendentals=0,
        ),
    )(*operands)


def add(*terms):
    total = terms[0].astype(F32)
    for term in terms[1:]:
        total = total + term.astype(F32)
    return total


def across_cores(value):
    return lax.ppermute(value, "outer", [(0, 1), (1, 0)])


def pair_sums(keep, got, chips):
    return [add(keep[0], got[0])] + [add(keep[k], got[k]).astype(BF) for k in range(1, chips)]


def to_owners(sums, chips):
    return [sums[0]] + [
        lax.ppermute(sums[k], "dp", [(i, i ^ k) for i in range(chips)]) for k in range(1, chips)
    ]


def mirror(sums, chips):
    devices = 2 * chips
    tile = BLK // devices
    return [
        lax.ppermute(
            sums[:, :, k * tile : (k + 1) * tile].astype(BF),
            ("dp", "outer"),
            [(i, (i + k) % devices) for i in range(devices)],
        )
        for k in range(1, chips)
    ]


def finish(where, priors, sums, mirrored, chips, token_total, after):
    devices = 2 * chips
    tile = BLK // devices
    counts = [prior.shape[0] for prior in priors]

    def body(where_ref, *rest):
        prior_refs, sums_ref, mirror_refs = rest[:2], rest[2], rest[3 : 2 + chips]
        outs = rest[-4:]
        me = where_ref[0] * 2 + where_ref[1]

        def one(prior_ref, stat_ref, new_ref):
            def put(at, total):
                columns = pl.ds(pl.multiple_of(lax.rem(me + at, devices) * tile, tile), tile)
                stat = total * (1.0 / token_total)
                stat_ref[0, :, columns] = stat
                new_ref[0, :, columns] = EMA_DECAY * prior_ref[0, :, columns] + (1.0 - EMA_DECAY) * stat

            for k in range(chips + 1):
                put(k, sums_ref[0, :, k * tile : (k + 1) * tile])
            for k in range(1, chips):
                put(devices - k, jnp.transpose(mirror_refs[k - 1][0].astype(F32)))

        first = pl.program_id(0) < counts[0]
        pl.when(first)(lambda: one(prior_refs[0], outs[0], outs[1]))
        pl.when(jnp.logical_not(first))(lambda: one(prior_refs[1], outs[2], outs[3]))

    early = pl.BlockSpec((1, tile, BLK), lambda b: (jnp.minimum(b, counts[0] - 1), 0, 0))
    late = pl.BlockSpec((1, tile, BLK), lambda b: (jnp.maximum(b - counts[0], 0), 0, 0))
    part = pl.BlockSpec((1, tile, tile * (chips + 1)), lambda b: (b, 0, 0))
    square = pl.BlockSpec((1, tile, tile), lambda b: (b, 0, 0))
    shapes = [jax.ShapeDtypeStruct(prior.shape, F32) for prior in priors]
    operands, specs = order_after(
        [where, *priors, sums, *mirrored],
        [pl.BlockSpec(memory_space=pltpu.SMEM), early, late, part] + [square] * (chips - 1),
        after,
    )
    return pl.pallas_call(
        body,
        grid=(sum(counts),),
        out_shape=(shapes[0], shapes[0], shapes[1], shapes[1]),
        in_specs=specs,
        out_specs=(early, early, late, late),
        compiler_params=pltpu.CompilerParams(vmem_limit_bytes=VMEM_LIMIT),
        cost_estimate=pl.CostEstimate(
            flops=4 * sum(counts) * tile * BLK,
            bytes_accessed=16 * sum(counts) * tile * BLK,
            transcendentals=0,
        ),
    )(*operands)


def plain_statistics(activations, act_scale, out_grads, gradient_tile_scale, prior_input_factor, g_factor):
    a_tiles = dequantize(activations, act_scale).reshape(activations.shape[0], -1, BLK)
    g_tiles = dequantize(out_grads, gradient_tile_scale).reshape(out_grads.shape[0], -1, BLK)
    inputs = a_tiles.shape[1]
    tiles = jnp.concatenate([a_tiles, g_tiles], axis=1)
    rows = jnp.einsum("qym,qyx->myx", tiles, tiles, preferred_element_type=F32)
    summed = lax.psum_scatter(
        rows.astype(BF), ("dp", "outer"), scatter_dimension=0, tiled=True
    ).astype(F32)
    token_total = activations.shape[0] * lax.axis_size("dp") * lax.axis_size("outer")
    statistics = jnp.transpose(summed, (1, 0, 2)) / token_total
    a_stat, g_stat = statistics[:inputs], statistics[inputs:]
    new_a_factor = EMA_DECAY * prior_input_factor + (1.0 - EMA_DECAY) * a_stat
    new_g_factor = EMA_DECAY * g_factor + (1.0 - EMA_DECAY) * g_stat
    return a_stat, g_stat, new_a_factor, new_g_factor


def left_product(where, pieces, weight_grad):
    rows, columns = weight_grad.shape
    step = min(512, columns)
    steps = columns // step
    blocks = rows // BLK
    cores = len(pieces[0])
    flat = [piece for group in pieces for piece in group]
    depth = flat[0].shape[1]

    def body(where_ref, w_ref, *rest):
        piece_refs = rest[: len(flat)]
        o_ref, a, w, out, a_sems, sems = rest[len(flat) :]

        def weights(i, n):
            return pltpu.make_async_copy(
                w_ref.at[pl.ds(i * BLK, BLK), pl.ds(n * step, step)],
                w.at[i, :, pl.ds(n * step, step)],
                sems.at[0, i, n],
            )

        def results(i, n):
            return pltpu.make_async_copy(
                out.at[i, :, pl.ds(n * step, step)],
                o_ref.at[pl.ds(i * BLK, BLK), pl.ds(n * step, step)],
                sems.at[1, i, n],
            )

        for i in range(blocks):
            for at, ref in enumerate(piece_refs):
                chip = jnp.bitwise_xor(where_ref[0], at // cores)
                core = jnp.bitwise_xor(where_ref[1], at % cores)
                start = pl.multiple_of((chip * cores + core) * depth, depth) if len(flat) > 1 else 0
                pltpu.make_async_copy(ref.at[i], a.at[i, pl.ds(start, depth)], a_sems.at[i]).start()
            if i == 0:
                weights(0, 0).start()
        order = [(i, n) for i in range(blocks) for n in range(steps)]
        weights(*order[1 % len(order)]).start()
        for i in range(blocks):
            pltpu.make_async_copy(a.at[i], a.at[i], a_sems.at[i]).wait()
            for n in range(steps):
                columns_of = slice(n * step, (n + 1) * step)
                weights(i, n).wait()
                if i * steps + n + 2 < len(order):
                    weights(*order[i * steps + n + 2]).start()
                out[i, :, columns_of] = jnp.dot(
                    a[i], w[i, :, columns_of], preferred_element_type=F32
                ).astype(BF)
                results(i, n).start()
        for i in range(blocks):
            for n in range(steps):
                results(i, n).wait()

    anywhere = pl.BlockSpec(memory_space=pl.ANY)
    return pl.pallas_call(
        body,
        out_shape=jax.ShapeDtypeStruct((rows, columns), BF),
        in_specs=[pl.BlockSpec(memory_space=pltpu.SMEM)] + [anywhere] * (1 + len(flat)),
        out_specs=anywhere,
        scratch_shapes=[
            pltpu.VMEM((blocks, BLK, BLK), BF),
            pltpu.VMEM((blocks, BLK, columns), BF),
            pltpu.VMEM((blocks, BLK, columns), BF),
            pltpu.SemaphoreType.DMA((blocks,)),
            pltpu.SemaphoreType.DMA((2, blocks, steps)),
        ],
        compiler_params=pltpu.CompilerParams(vmem_limit_bytes=VMEM_LIMIT),
        cost_estimate=pl.CostEstimate(
            flops=int(4.0 * rows * columns * BLK),
            bytes_accessed=int(4 * rows * columns),
            transcendentals=0,
        ),
    )(where, weight_grad, *flat)


def tie(value, *after):
    return lax.optimization_barrier((value, *after))[0] if after else value


def right_product(left, inverses):
    rows, columns = left.shape
    blocks = columns // BLK
    step = 512
    steps = rows // step

    def body(left_ref, inverse_ref, o_ref, right, a, out, r_sems, sems):
        def inverse(block):
            return pltpu.make_async_copy(inverse_ref.at[block], right.at[block], r_sems.at[block])

        def incoming(block, n):
            return pltpu.make_async_copy(
                left_ref.at[pl.ds(n * step, step), pl.ds(block * BLK, BLK)],
                a.at[block, pl.ds(n * step, step)],
                sems.at[0, block, n],
            )

        def outgoing(block, n):
            return pltpu.make_async_copy(
                out.at[block, pl.ds(n * step, step)],
                o_ref.at[pl.ds(n * step, step), pl.ds(block * BLK, BLK)],
                sems.at[1, block, n],
            )

        order = [(block, n) for block in range(blocks) for n in range(steps)]
        inverse(0).start()
        for at in order[:2]:
            incoming(*at).start()
        for block in range(blocks):
            inverse(block).wait()
            if block + 1 < blocks:
                inverse(block + 1).start()
            for n in range(steps):
                incoming(block, n).wait()
                if block * steps + n + 2 < len(order):
                    incoming(*order[block * steps + n + 2]).start()
                rows_of = slice(n * step, (n + 1) * step)
                out[block, rows_of, :] = jnp.dot(
                    a[block, rows_of, :], right[block], preferred_element_type=F32
                ).astype(BF)
                outgoing(block, n).start()
        for block in range(blocks):
            for n in range(steps):
                outgoing(block, n).wait()

    anywhere = pl.BlockSpec(memory_space=pl.ANY)
    return pl.pallas_call(
        body,
        out_shape=jax.ShapeDtypeStruct((rows, columns), BF),
        in_specs=[anywhere, anywhere],
        out_specs=anywhere,
        scratch_shapes=[
            pltpu.VMEM((blocks, BLK, BLK), BF),
            pltpu.VMEM((blocks, rows, BLK), BF),
            pltpu.VMEM((blocks, rows, BLK), BF),
            pltpu.SemaphoreType.DMA((blocks,)),
            pltpu.SemaphoreType.DMA((2, blocks, steps)),
        ],
        compiler_params=pltpu.CompilerParams(vmem_limit_bytes=VMEM_LIMIT),
        cost_estimate=pl.CostEstimate(
            flops=int(4.0 * rows * columns * BLK),
            bytes_accessed=4 * rows * columns + 2 * columns * BLK,
            transcendentals=0,
        ),
    )(left, inverses)


def body(
    activations,
    act_scale,
    out_grads,
    gradient_tile_scale,
    prior_input_factor,
    g_factor,
    weight_grad,
    a_inverse,
    g_inverse,
):
    chips = lax.axis_size("dp")
    devices = chips * lax.axis_size("outer")
    where = jnp.stack([lax.axis_index("dp"), lax.axis_index("outer")]).astype(jnp.int32)
    inverses = lax.all_gather(g_inverse, "mp", axis=1, tiled=True)

    symmetric = (
        lax.axis_size("outer") == 2
        and chips >= 2
        and chips & (chips - 1) == 0
        and BLK // devices % QT == 0
        and activations.shape[1] + out_grads.shape[1] > 2 * BLK
    )
    if not symmetric:
        stats = plain_statistics(
            activations, act_scale, out_grads, gradient_tile_scale, prior_input_factor, g_factor
        )
        a_blocks = lax.all_gather(a_inverse, ("dp", "outer"), axis=1, tiled=True)
        left = left_product(where, [[a_blocks]], weight_grad)
        return (*stats, right_product(left, inverses))

    panels = [out_grads, activations]
    scales = [gradient_tile_scale, act_scale]
    blocks = [(p, b) for p in range(2) for b in range(panels[p].shape[1] // BLK)]
    chunks = [blocks[at : at + 2] for at in range(0, len(blocks), 2)]

    gathered = [a_inverse] + [
        lax.ppermute(a_inverse, "dp", [(i, i ^ k) for i in range(chips)]) for k in range(1, chips)
    ]
    keep, got, terms = [], [], []
    for n, chunk in enumerate(chunks):
        here = where
        if n == 1:
            here = tie(where, keep[0])
        elif n > 1:
            ready = pair_sums(keep[n - 2], got[n - 2], chips)
            here = tie(where, keep[n - 1], *ready[1:], *gathered)
            terms.append(to_owners(ready, chips))
        kept, sent = gram_blocks(here, panels, scales, chunk, chips, ())
        keep.append(kept)
        got.append(across_cores(sent))
    pieces = [[piece, across_cores(tie(piece, keep[-2]))] for piece in gathered]
    ready = pair_sums(keep[-2], got[-2], chips)
    left = left_product(tie(where, keep[-1], *ready[1:]), pieces, weight_grad)
    terms.append(to_owners(ready, chips))
    terms.append(to_owners(pair_sums(keep[-1], got[-1], chips), chips))
    sums = jnp.concatenate([add(*some) for some in terms])
    mirrored = mirror(sums, chips)
    token_total = activations.shape[0] * devices
    result = right_product(tie(left, sums), inverses)
    where = tie(where, result)
    g_stat, new_g_factor, a_stat, new_a_factor = finish(
        where, [g_factor, prior_input_factor], sums, mirrored, chips, token_total, ()
    )
    return a_stat, g_stat, new_a_factor, new_g_factor, result


def solution(mesh):
    return jax.shard_map(
        body,
        mesh=mesh,
        in_specs=(
            P(("dp", "outer"), "mp"),
            P(("dp", "outer"), "mp"),
            P(("dp", "outer"), "mp"),
            P(("dp", "outer"), "mp"),
            P("mp", ("dp", "outer"), None),
            P("mp", ("dp", "outer"), None),
            P("mp", ("dp", "outer")),
            P("mp", ("dp", "outer"), None),
            P(("dp", "outer"), "mp", None),
        ),
        out_specs=(
            P("mp", ("dp", "outer"), None),
            P("mp", ("dp", "outer"), None),
            P("mp", ("dp", "outer"), None),
            P("mp", ("dp", "outer"), None),
            P("mp", ("dp", "outer")),
        ),
        check_vma=False,
    )
```

```python
import jax
import jax.numpy as jnp
from jax import lax
from jax.experimental import pallas as pl
from jax.experimental.pallas import tpu as pltpu
from jax.sharding import PartitionSpec as P

BLK = 1024
QT = 128
EMA_DECAY = 0.95
BF = jnp.bfloat16
F32 = jnp.float32
VMEM_LIMIT = 60 * 1024 * 1024


def dequantize(quantized, tile_scale):
    rows, columns = quantized.shape
    tiles = (
        quantized.reshape(rows // QT, QT, columns // QT, QT).astype(F32)
        * tile_scale[:, None, :, None]
    )
    return tiles.reshape(rows, columns).astype(BF)


def order_after(operands, specs, after):
    for value in after:
        operands.append(value)
        specs.append(pl.BlockSpec(memory_space=pl.ANY))
    return operands, specs


def gram_blocks(where, panels, scales, blocks, chips, after):
    tokens = panels[0].shape[0]
    pair = BLK // chips
    tile = pair // 2
    half = chips // 2
    width = tile * (chips + 1)
    count = len(blocks)
    parts = chips if tokens % (chips * QT) == 0 else 1
    depth = tokens // parts
    wide = BLK + half * pair

    def body(where_ref, *rest):
        scale_refs, panel_refs = rest[:2], rest[2:4]
        keep_hbm, send_hbm, raw, rows_out, in_sems, out_sems = rest[4 + len(after) : -2]
        deq = rest[-2:]

        def incoming(n, part):
            panel, block = blocks[n]
            return pltpu.make_async_copy(
                panel_refs[panel].at[pl.ds(part * depth, depth), pl.ds(block * BLK, BLK)],
                raw.at[n, pl.ds(part * depth, depth)],
                in_sems.at[n, part],
            )

        def outgoing(n):
            return (
                pltpu.make_async_copy(rows_out.at[0, n], keep_hbm.at[:, n], out_sems.at[n, 0]),
                pltpu.make_async_copy(rows_out.at[1, n], send_hbm.at[:, n], out_sems.at[n, 1]),
            )

        def convert(n, part):
            panel, block = blocks[n]
            into = deq[n % 2]
            for t in range(part * depth // QT, (part + 1) * depth // QT):
                rows = slice(t * QT, (t + 1) * QT)
                for u in range(BLK // QT):
                    factor = scale_refs[panel][t, block * (BLK // QT) + u]
                    value = (raw[n, rows, u * QT : (u + 1) * QT].astype(F32) * factor).astype(BF)
                    into[rows, u * QT : (u + 1) * QT] = value
                    if u * QT < wide - BLK:
                        into[rows, BLK + u * QT : BLK + (u + 1) * QT] = value

        for part in range(parts):
            incoming(0, part).start()
        for part in range(parts):
            incoming(0, part).wait()
            convert(0, part)
            if count > 1:
                incoming(1, part).start()
        for n in range(count):
            if 0 < n < count - 1:
                for part in range(parts):
                    incoming(n + 1, part).start()
            source = deq[n % 2]
            far = []
            for chip in range(chips):
                span = half * pair + (pair if chip < half else 0)
                start = chip * pair
                if n + 1 < count and chip < parts:
                    incoming(n + 1, chip).wait()
                sums = lax.dot_general(
                    source[:, start : start + pair],
                    source[:, start : start + span],
                    (((0,), (0,)), ((), ())),
                    preferred_element_type=F32,
                )
                if n + 1 < count and chip < parts:
                    convert(n + 1, chip)
                near = sums[:, : half * pair].astype(BF)
                if chip < half:
                    last = sums[:, half * pair :].astype(BF)
                    far.append(last)
                else:
                    last = jnp.transpose(far[chip - half])
                place = jnp.bitwise_xor(where_ref[0], chip)

                for core in range(2):
                    side = jnp.bitwise_xor(where_ref[1], core)
                    rows = slice(core * tile, (core + 1) * tile)
                    cut = half * pair - core * tile
                    rows_out[side, n, place, :, :cut] = near[rows, core * tile :]
                    rows_out[side, n, place, :, cut:] = last[rows, : (core + 1) * tile]

            for copy in outgoing(n):
                copy.start()
        for n in range(count):
            for copy in outgoing(n):
                copy.wait()

    shape = jax.ShapeDtypeStruct((chips, count, tile, width), BF)
    anywhere = pl.BlockSpec(memory_space=pl.ANY)
    operands, specs = order_after(
        [where, *scales, *panels],
        [pl.BlockSpec(memory_space=pltpu.SMEM)] * 3 + [anywhere] * 2,
        after,
    )
    return pl.pallas_call(
        body,
        out_shape=(shape, shape),
        in_specs=specs,
        out_specs=(anywhere, anywhere),
        scratch_shapes=[
            pltpu.VMEM((count, tokens, BLK), BF),
            pltpu.VMEM((2, count, chips, tile, width), BF),
            pltpu.SemaphoreType.DMA((count, parts)),
            pltpu.SemaphoreType.DMA((count, 2)),
            pltpu.VMEM((tokens, wide), BF),
            pltpu.VMEM((tokens, wide), BF),
        ],
        compiler_params=pltpu.CompilerParams(vmem_limit_bytes=VMEM_LIMIT),
        cost_estimate=pl.CostEstimate(
            flops=(6 if count > 1 else 2) * count * tokens * BLK * width,
            bytes_accessed=2 * count * (tokens * BLK + 2 * chips * tile * width),
            transcendentals=0,
        ),
    )(*operands)


def add(*terms):
    total = terms[0].astype(F32)
    for term in terms[1:]:
        total = total + term.astype(F32)
    return total


def across_cores(value):
    return lax.ppermute(value, "outer", [(0, 1), (1, 0)])


def pair_sums(keep, got, chips):
    return [add(keep[0], got[0])] + [add(keep[k], got[k]).astype(BF) for k in range(1, chips)]


def to_owners(sums, chips):
    return [sums[0]] + [
        lax.ppermute(sums[k], "dp", [(i, i ^ k) for i in range(chips)]) for k in range(1, chips)
    ]


def mirror(sums, chips):
    devices = 2 * chips
    tile = BLK // devices
    return [
        lax.ppermute(
            sums[:, :, k * tile : (k + 1) * tile].astype(BF),
            ("dp", "outer"),
            [(i, (i + k) % devices) for i in range(devices)],
        )
        for k in range(1, chips)
    ]


def finish(where, priors, sums, mirrored, chips, token_total, after):
    devices = 2 * chips
    tile = BLK // devices
    counts = [prior.shape[0] for prior in priors]

    def body(where_ref, *rest):
        prior_refs, sums_ref, mirror_refs = rest[:2], rest[2], rest[3 : 2 + chips]
        outs = rest[-4:]
        me = where_ref[0] * 2 + where_ref[1]

        def one(prior_ref, stat_ref, new_ref):
            def put(at, total):
                columns = pl.ds(pl.multiple_of(lax.rem(me + at, devices) * tile, tile), tile)
                stat = total * (1.0 / token_total)
                stat_ref[0, :, columns] = stat
                new_ref[0, :, columns] = EMA_DECAY * prior_ref[0, :, columns] + (1.0 - EMA_DECAY) * stat

            for k in range(chips + 1):
                put(k, sums_ref[0, :, k * tile : (k + 1) * tile])
            for k in range(1, chips):
                put(devices - k, jnp.transpose(mirror_refs[k - 1][0].astype(F32)))

        first = pl.program_id(0) < counts[0]
        pl.when(first)(lambda: one(prior_refs[0], outs[0], outs[1]))
        pl.when(jnp.logical_not(first))(lambda: one(prior_refs[1], outs[2], outs[3]))

    early = pl.BlockSpec((1, tile, BLK), lambda b: (jnp.minimum(b, counts[0] - 1), 0, 0))
    late = pl.BlockSpec((1, tile, BLK), lambda b: (jnp.maximum(b - counts[0], 0), 0, 0))
    part = pl.BlockSpec((1, tile, tile * (chips + 1)), lambda b: (b, 0, 0))
    square = pl.BlockSpec((1, tile, tile), lambda b: (b, 0, 0))
    shapes = [jax.ShapeDtypeStruct(prior.shape, F32) for prior in priors]
    operands, specs = order_after(
        [where, *priors, sums, *mirrored],
        [pl.BlockSpec(memory_space=pltpu.SMEM), early, late, part] + [square] * (chips - 1),
        after,
    )
    return pl.pallas_call(
        body,
        grid=(sum(counts),),
        out_shape=(shapes[0], shapes[0], shapes[1], shapes[1]),
        in_specs=specs,
        out_specs=(early, early, late, late),
        compiler_params=pltpu.CompilerParams(vmem_limit_bytes=VMEM_LIMIT),
        cost_estimate=pl.CostEstimate(
            flops=4 * sum(counts) * tile * BLK,
            bytes_accessed=16 * sum(counts) * tile * BLK,
            transcendentals=0,
        ),
    )(*operands)


def plain_statistics(activations, act_scale, out_grads, gradient_tile_scale, prior_input_factor, g_factor):
    a_tiles = dequantize(activations, act_scale).reshape(activations.shape[0], -1, BLK)
    g_tiles = dequantize(out_grads, gradient_tile_scale).reshape(out_grads.shape[0], -1, BLK)
    inputs = a_tiles.shape[1]
    tiles = jnp.concatenate([a_tiles, g_tiles], axis=1)
    rows = jnp.einsum("qym,qyx->myx", tiles, tiles, preferred_element_type=F32)
    summed = lax.psum_scatter(
        rows.astype(BF), ("dp", "outer"), scatter_dimension=0, tiled=True
    ).astype(F32)
    token_total = activations.shape[0] * lax.axis_size("dp") * lax.axis_size("outer")
    statistics = jnp.transpose(summed, (1, 0, 2)) / token_total
    a_stat, g_stat = statistics[:inputs], statistics[inputs:]
    new_a_factor = EMA_DECAY * prior_input_factor + (1.0 - EMA_DECAY) * a_stat
    new_g_factor = EMA_DECAY * g_factor + (1.0 - EMA_DECAY) * g_stat
    return a_stat, g_stat, new_a_factor, new_g_factor


def left_product(where, pieces, weight_grad):
    rows, columns = weight_grad.shape
    step = min(512, columns)
    steps = columns // step
    blocks = rows // BLK
    cores = len(pieces[0])
    flat = [piece for group in pieces for piece in group]
    depth = flat[0].shape[1]

    def body(where_ref, w_ref, *rest):
        piece_refs = rest[: len(flat)]
        o_ref, a, w, out, a_sems, sems = rest[len(flat) :]

        def weights(i, n):
            return pltpu.make_async_copy(
                w_ref.at[pl.ds(i * BLK, BLK), pl.ds(n * step, step)],
                w.at[i, :, pl.ds(n * step, step)],
                sems.at[0, i, n],
            )

        def results(i, n):
            return pltpu.make_async_copy(
                out.at[i, :, pl.ds(n * step, step)],
                o_ref.at[pl.ds(i * BLK, BLK), pl.ds(n * step, step)],
                sems.at[1, i, n],
            )

        for i in range(blocks):
            for at, ref in enumerate(piece_refs):
                chip = jnp.bitwise_xor(where_ref[0], at // cores)
                core = jnp.bitwise_xor(where_ref[1], at % cores)
                start = pl.multiple_of((chip * cores + core) * depth, depth) if len(flat) > 1 else 0
                pltpu.make_async_copy(ref.at[i], a.at[i, pl.ds(start, depth)], a_sems.at[i]).start()
            if i == 0:
                weights(0, 0).start()
        order = [(i, n) for i in range(blocks) for n in range(steps)]
        weights(*order[1 % len(order)]).start()
        for i in range(blocks):
            pltpu.make_async_copy(a.at[i], a.at[i], a_sems.at[i]).wait()
            for n in range(steps):
                columns_of = slice(n * step, (n + 1) * step)
                weights(i, n).wait()
                if i * steps + n + 2 < len(order):
                    weights(*order[i * steps + n + 2]).start()
                out[i, :, columns_of] = jnp.dot(
                    a[i], w[i, :, columns_of], preferred_element_type=F32
                ).astype(BF)
                results(i, n).start()
        for i in range(blocks):
            for n in range(steps):
                results(i, n).wait()

    anywhere = pl.BlockSpec(memory_space=pl.ANY)
    return pl.pallas_call(
        body,
        out_shape=jax.ShapeDtypeStruct((rows, columns), BF),
        in_specs=[pl.BlockSpec(memory_space=pltpu.SMEM)] + [anywhere] * (1 + len(flat)),
        out_specs=anywhere,
        scratch_shapes=[
            pltpu.VMEM((blocks, BLK, BLK), BF),
            pltpu.VMEM((blocks, BLK, columns), BF),
            pltpu.VMEM((blocks, BLK, columns), BF),
            pltpu.SemaphoreType.DMA((blocks,)),
            pltpu.SemaphoreType.DMA((2, blocks, steps)),
        ],
        compiler_params=pltpu.CompilerParams(vmem_limit_bytes=VMEM_LIMIT),
        cost_estimate=pl.CostEstimate(
            flops=int(2.4 * rows * columns * BLK),
            bytes_accessed=int(4 * rows * columns),
            transcendentals=0,
        ),
    )(where, weight_grad, *flat)


def tie(value, *after):
    return lax.optimization_barrier((value, *after))[0] if after else value


def right_product(left, inverses):
    rows, columns = left.shape
    blocks = columns // BLK
    step = 512
    steps = rows // step

    def body(left_ref, inverse_ref, o_ref, right, a, out, r_sems, sems):
        def inverse(block):
            return pltpu.make_async_copy(inverse_ref.at[block], right.at[block], r_sems.at[block])

        def incoming(block, n):
            return pltpu.make_async_copy(
                left_ref.at[pl.ds(n * step, step), pl.ds(block * BLK, BLK)],
                a.at[block, pl.ds(n * step, step)],
                sems.at[0, block, n],
            )

        def outgoing(block, n):
            return pltpu.make_async_copy(
                out.at[block, pl.ds(n * step, step)],
                o_ref.at[pl.ds(n * step, step), pl.ds(block * BLK, BLK)],
                sems.at[1, block, n],
            )

        order = [(block, n) for block in range(blocks) for n in range(steps)]
        inverse(0).start()
        for at in order[:2]:
            incoming(*at).start()
        for block in range(blocks):
            inverse(block).wait()
            if block + 1 < blocks:
                inverse(block + 1).start()
            for n in range(steps):
                incoming(block, n).wait()
                if block * steps + n + 2 < len(order):
                    incoming(*order[block * steps + n + 2]).start()
                rows_of = slice(n * step, (n + 1) * step)
                out[block, rows_of, :] = jnp.dot(
                    a[block, rows_of, :], right[block], preferred_element_type=F32
                ).astype(BF)
                outgoing(block, n).start()
        for block in range(blocks):
            for n in range(steps):
                outgoing(block, n).wait()

    anywhere = pl.BlockSpec(memory_space=pl.ANY)
    return pl.pallas_call(
        body,
        out_shape=jax.ShapeDtypeStruct((rows, columns), BF),
        in_specs=[anywhere, anywhere],
        out_specs=anywhere,
        scratch_shapes=[
            pltpu.VMEM((blocks, BLK, BLK), BF),
            pltpu.VMEM((blocks, rows, BLK), BF),
            pltpu.VMEM((blocks, rows, BLK), BF),
            pltpu.SemaphoreType.DMA((blocks,)),
            pltpu.SemaphoreType.DMA((2, blocks, steps)),
        ],
        compiler_params=pltpu.CompilerParams(vmem_limit_bytes=VMEM_LIMIT),
        cost_estimate=pl.CostEstimate(
            flops=int(4.0 * rows * columns * BLK),
            bytes_accessed=4 * rows * columns + 2 * columns * BLK,
            transcendentals=0,
        ),
    )(left, inverses)


def body(
    activations,
    act_scale,
    out_grads,
    gradient_tile_scale,
    prior_input_factor,
    g_factor,
    weight_grad,
    a_inverse,
    g_inverse,
):
    chips = lax.axis_size("dp")
    devices = chips * lax.axis_size("outer")
    where = jnp.stack([lax.axis_index("dp"), lax.axis_index("outer")]).astype(jnp.int32)
    inverses = lax.all_gather(g_inverse, "mp", axis=1, tiled=True)

    symmetric = (
        lax.axis_size("outer") == 2
        and chips >= 2
        and chips & (chips - 1) == 0
        and BLK // devices % QT == 0
        and activations.shape[1] + out_grads.shape[1] > 2 * BLK
    )
    if not symmetric:
        stats = plain_statistics(
            activations, act_scale, out_grads, gradient_tile_scale, prior_input_factor, g_factor
        )
        a_blocks = lax.all_gather(a_inverse, ("dp", "outer"), axis=1, tiled=True)
        left = left_product(where, [[a_blocks]], weight_grad)
        return (*stats, right_product(left, inverses))

    panels = [out_grads, activations]
    scales = [gradient_tile_scale, act_scale]
    blocks = [(p, b) for p in range(2) for b in range(panels[p].shape[1] // BLK)]
    half = (len(blocks) + 1) // 2
    rest = (len(blocks) - half + 1) // 2
    chunks = [blocks[:half], blocks[half : half + rest], blocks[half + rest :]]

    gathered = [a_inverse] + [
        lax.ppermute(a_inverse, "dp", [(i, i ^ k) for i in range(chips)]) for k in range(1, chips)
    ]
    keep, got, terms = [], [], []
    left = None
    for n, chunk in enumerate(chunks):
        here, arrived = where, ()
        if n == 1:
            here = tie(where, keep[0])
        elif n > 1:
            if left is None:
                ready = pair_sums(keep[n - 2], got[n - 2], chips)
                terms.append(to_owners(ready, chips))
                pieces = [[piece, across_cores(tie(piece, keep[0]))] for piece in gathered]
                left = left_product(tie(where, keep[n - 1], *ready[1:]), pieces, weight_grad)
            ready = pair_sums(tie(keep[n - 1], left), got[n - 1], chips)
            here = tie(where, left, *terms[-1][1:], *ready[1:])
            terms.append(to_owners(ready, chips))
            arrived = terms[-1][1:]
        kept, sent = gram_blocks(here, panels, scales, chunk, chips, ())
        keep.append(kept)
        got.append(across_cores(tie(sent, *arrived)))
    terms.append(to_owners(pair_sums(keep[-1], got[-1], chips), chips))
    sums = jnp.concatenate([add(*some) for some in terms])
    mirrored = mirror(sums, chips)
    token_total = activations.shape[0] * devices
    result = right_product(tie(left, sums), inverses)
    where = tie(where, result)
    g_stat, new_g_factor, a_stat, new_a_factor = finish(
        where, [g_factor, prior_input_factor], sums, mirrored, chips, token_total, ()
    )
    return a_stat, g_stat, new_a_factor, new_g_factor, result


def solution(mesh):
    return jax.shard_map(
        body,
        mesh=mesh,
        in_specs=(
            P(("dp", "outer"), "mp"),
            P(("dp", "outer"), "mp"),
            P(("dp", "outer"), "mp"),
            P(("dp", "outer"), "mp"),
            P("mp", ("dp", "outer"), None),
            P("mp", ("dp", "outer"), None),
            P("mp", ("dp", "outer")),
            P("mp", ("dp", "outer"), None),
            P(("dp", "outer"), "mp", None),
        ),
        out_specs=(
            P("mp", ("dp", "outer"), None),
            P("mp", ("dp", "outer"), None),
            P("mp", ("dp", "outer"), None),
            P("mp", ("dp", "outer"), None),
            P("mp", ("dp", "outer")),
        ),
        check_vma=False,
    )
```
